32 devices in a mesh: groups: 2 (over y), ep: 4 (over z), sub: 4 (over x, core).
Axes of the slice: x: 2, y: 2, z: 4, core: 2. Of those that a mesh axis runs over, the one named last changes fastest.
Arguments:
- tokens: bfloat16 [2048, 7168], P(('groups', 'ep', 'sub')), parts along dimension 0, may hold values from -6 to 6
- routes: int32 [2048, 8], P(('groups', 'ep', 'sub')), parts along dimension 0, may hold values from 0 to 255, as said below
- route_weights: float32 [2048, 8], P(('groups', 'ep', 'sub')), parts along dimension 0, may hold values from 0.5 to 2.5
- w_gate: bfloat16 [4, 7168, 2048], P('ep', None, 'sub'), may hold values from -0.0625 to 0.0625
- w_up: bfloat16 [4, 7168, 2048], P('ep', None, 'sub'), may hold values from -0.0625 to 0.0625
- w_down: bfloat16 [4, 2048, 7168], P('ep', 'sub'), may hold values from -0.125 to 0.125
Outputs:
- combined: bfloat16 [2048, 7168], P(('groups', 'ep', 'sub')), parts along dimension 0
The draws below stay inside these ranges and needn't reach their ends.
There are 2 independent parts, one for each index of `groups`. The reference program is written for one: setup_inputs(seed, part) draws one part's arguments, and reference() takes and returns one part's arrays. A program takes and returns all parts, laid end to end along the dimension named above; an argument that names none is the same for every part. Nothing has to cross between parts.
Inputs may be any that keep to these rules, and one draw needn't show every extreme that they name: `routes`: each row names 8 different experts and at most one expert below 4. In the 64 rows of one device every expert below 4 is named by 1 to 16 rows; in every draw one such expert is named by exactly 16 rows on every device.
All inputs are finite; a program needn't handle non-finite values.
Results may differ from the reference program's by a relative error of at most 0.0095.
Values may be sent and summed in bfloat16 or wider, within the bound.
A program may use at most 128 MiB of HBM per device.

```python
import jax
import jax.numpy as jnp
from jax import lax

D = 7168
EXPERTS = 256
TOPK = 8
H_WIN = 2048
TOK_DEV = 64
CAP = 16
EXP_FLIGHT = 4
TOKENS = 1024
N_SUB = 4


def draw_routes(key, part):
    key = jax.random.fold_in(key, 11)
    key_counts, key_full, key_order, key_scores, key_roll = jax.random.split(key, 5)
    blocks_count = TOKENS // TOK_DEV
    counts = jax.random.randint(key_counts, (blocks_count, EXP_FLIGHT), 1, CAP + 1)
    full_one = jax.random.randint(key_full, (), 0, EXP_FLIGHT)
    counts = jnp.where(jnp.arange(EXP_FLIGHT)[None, :] == full_one, CAP, counts)
    ends = jnp.cumsum(counts, axis=1)
    totals = ends[:, -1:]
    order_keys = jax.random.split(key_order, blocks_count)
    places = jax.vmap(lambda single: jax.random.permutation(single, TOK_DEV))(order_keys)
    flight_of = jnp.sum((places[:, :, None] >= ends[:, None, :]).astype(jnp.int32), axis=2)
    assigned = places < totals
    others_count = EXPERTS - EXP_FLIGHT
    scores = jax.random.randint(key_scores, (TOKENS, others_count), 0, 1 << 20) * others_count + jnp.arange(others_count)[None, :]
    top_scores, picked = lax.top_k(scores, TOPK)
    others = EXP_FLIGHT + picked
    first = jnp.where(assigned.reshape(TOKENS), flight_of.reshape(TOKENS), others[:, TOPK - 1])
    listed = jnp.concatenate([first[:, None], others[:, :TOPK - 1]], axis=1)
    shift = jax.random.randint(key_roll, (TOKENS, 1), 0, TOPK)
    where_from = (jnp.arange(TOPK)[None, :] + shift) % TOPK
    return jnp.take_along_axis(listed, where_from, axis=1).astype(jnp.int32)


def level_of(key, shape, cuts, low, largest):
    def one(dim, shards_of):
        steps = jax.random.uniform(jax.random.fold_in(jax.random.fold_in(key, 6), dim), (shards_of,), jnp.float32, low / len(cuts), largest / len(cuts))
        return jnp.repeat(jnp.exp(steps), shape[dim] // shards_of).reshape((-1,) + (1,) * (len(shape) - dim - 1))

    factor_of = one(*cuts[0])
    for cut in cuts[1:]:
        factor_of = factor_of * one(*cut)
    return factor_of


def centred(key, extent, deviation, reach, cuts=(), kind=jnp.bfloat16):
    result = deviation * jax.random.normal(key, extent, jnp.float32)
    if cuts:
        result = result * level_of(key, extent, cuts, -0.22, 0.18)
    return jnp.clip(result, -reach, reach).astype(kind)


def setup_inputs(seed: int = 0, part: int = 0) -> dict:
    key_list = jax.random.split(jax.random.key(seed), 7)
    part_splits = jax.random.split(jax.random.fold_in(key_list[6], part), 7)
    return {
        "tokens": centred(part_splits[0], (TOKENS, D), 1.0, 6.0, ((0, 16),)),
        "routes": draw_routes(jax.random.fold_in(jax.random.fold_in(key_list[6], part), 71), part),
        "route_weights": jnp.clip(0.5 + 2.0 * jax.random.uniform(part_splits[2], (TOKENS, TOPK), jnp.float32) ** level_of(part_splits[2], (TOKENS, TOPK), ((0, 16),), -0.2, 0.2), 0.5, 2.5),
        "w_gate": centred(key_list[3], (EXP_FLIGHT, D, H_WIN), D ** -0.5, 0.0625, ((0, 4), (2, 4))),
        "w_up": centred(key_list[4], (EXP_FLIGHT, D, H_WIN), D ** -0.5, 0.0625, ((0, 4), (2, 4))),
        "w_down": centred(key_list[5], (EXP_FLIGHT, H_WIN, D), H_WIN ** -0.5, 0.125, ((0, 4), (1, 4))),
    }


def settle(values):
    return lax.optimization_barrier(values)


def reference(tokens, routes, route_weights, w_gate, w_up, w_down):
    blocks_count = TOKENS // TOK_DEV
    hits = routes[:, :, None] == jnp.arange(EXP_FLIGHT, dtype=jnp.int32)[None, None, :]
    chosen = jnp.any(hits, axis=1)
    weight_of = jnp.sum(jnp.where(hits, route_weights[:, :, None], jnp.zeros((), jnp.float32)), axis=1).astype(jnp.float32)
    flags = chosen.astype(jnp.int32).reshape(blocks_count, TOK_DEV, EXP_FLIGHT)
    slots = (jnp.cumsum(flags, axis=1) - flags).reshape(TOKENS, EXP_FLIGHT)
    row_ids = jnp.arange(TOKENS, dtype=jnp.int32)
    spare = blocks_count * CAP
    target = jnp.where(chosen, (row_ids // TOK_DEV)[:, None] * CAP + slots, spare).astype(jnp.int32)
    group = H_WIN // N_SUB

    def one_expert(running, pieces):
        gate_w, up_w, down_w, target_row, factor = pieces
        table = jnp.zeros((spare + 1,), jnp.int32).at[target_row].set(row_ids)
        filled = jnp.zeros((spare + 1,), jnp.bool_).at[target_row].set(True)
        inputs = jnp.where(filled[:spare, None], tokens[table[:spare]], jnp.zeros((), jnp.bfloat16))
        gate = jnp.dot(inputs, gate_w, preferred_element_type=jnp.float32)
        up = jnp.dot(inputs, up_w, preferred_element_type=jnp.float32)
        hidden = (jax.nn.silu(gate) * up).astype(jnp.bfloat16)
        summed = jnp.zeros((spare, D), jnp.float32)
        for portion in range(N_SUB):
            lower = portion * group
            product = jnp.dot(hidden[:, lower:lower + group], down_w[lower:lower + group], preferred_element_type=jnp.float32)
            summed = summed + settle(product.astype(jnp.bfloat16)).astype(jnp.float32)
        outcome = summed.astype(jnp.bfloat16)
        padded = jnp.concatenate([outcome, jnp.zeros((1, D), jnp.bfloat16)], axis=0)
        running = running + factor[:, None] * settle(padded[target_row]).astype(jnp.float32)
        return running, None

    start = jnp.zeros((TOKENS, D), jnp.float32)
    running, ignored = lax.scan(one_expert, start, (w_gate, w_up, w_down, target.T, weight_of.T))
    return running.astype(jnp.bfloat16)
```

```python
import functools

import jax
import jax.numpy as jnp
from jax import lax
from jax.experimental import pallas as pl
from jax.experimental.pallas import tpu as pltpu
from jax.sharding import PartitionSpec as P

MESH = pl.DeviceIdType.MESH


def settle(values):
    return lax.optimization_barrier(values)


def flip(index, step, extent):
    result = 0
    bit = 1
    while bit < extent:
        digit = lax.rem(lax.div(index, bit), 2)
        result = result + (1 - digit if step & bit else digit) * bit
        bit *= 2
    return result


def layer_kernel(
    n_major,
    cap,
    tile,
    tokens_ref,
    routes_ref,
    weights_ref,
    gate_hbm,
    up_hbm,
    down_hbm,
    out_ref,
    gate_w,
    up_w,
    down_w,
    outgoing,
    rows_in,
    partial,
    core_in,
    x_out,
    x_in,
    z_out,
    returned,
    gate_acc,
    up_acc,
    w_sem,
    dz_send,
    dz_recv,
    dx_send,
    dx_recv,
    dc_send,
    dc_recv,
    rc_send,
    rc_recv,
    rx_send,
    rx_recv,
    rz_send,
    rz_recv,
):
    rows, width = tokens_ref.shape
    slots = n_major * cap
    chunk = 4 * cap
    e = lax.axis_index("ep")
    s = lax.axis_index("sub")
    x = lax.div(s, 2)
    c = lax.rem(s, 2)
    s_core = 2 * x + (1 - c)
    s_x = 2 * (1 - x) + c
    s_far = 2 * (1 - x) + (1 - c)
    planes = [flip(e, k, n_major) for k in range(n_major)]

    loads = [
        pltpu.make_async_copy(gate_hbm.at[0], gate_w, w_sem.at[0]),
        pltpu.make_async_copy(up_hbm.at[0], up_w, w_sem.at[1]),
        pltpu.make_async_copy(down_hbm.at[0], down_w, w_sem.at[2]),
    ]
    for load in loads:
        load.start()

    barrier = pltpu.get_barrier_semaphore()
    partners = [(planes[k], s) for k in range(1, n_major)] + [(e, s_x), (e, s_core)]
    for plane, sub in partners:
        pl.semaphore_signal(
            barrier, inc=1, device_id={"ep": plane, "sub": sub}, device_id_type=MESH
        )

    def selector_of():
        column = lax.broadcasted_iota(jnp.int32, (rows, slots), 1)
        expert = lax.div(column, cap)
        place = lax.rem(column, cap)
        chosen = jnp.zeros((rows, slots), jnp.float32)
        for k in range(routes_ref.shape[1]):
            chosen = jnp.maximum(
                chosen, jnp.where(routes_ref[:, k : k + 1] == expert, 1.0, 0.0)
            )
        earlier = jnp.where(
            lax.broadcasted_iota(jnp.int32, (rows, rows), 0)
            > lax.broadcasted_iota(jnp.int32, (rows, rows), 1),
            1.0,
            0.0,
        ).astype(jnp.bfloat16)
        slot = jnp.dot(earlier, chosen.astype(jnp.bfloat16), preferred_element_type=jnp.float32)
        return jnp.where(slot == place.astype(jnp.float32), chosen, 0.0).astype(jnp.bfloat16)

    selector = selector_of()

    @pl.loop(0, width // tile)
    def _(j):
        cols = pl.ds(pl.multiple_of(j * tile, tile), tile)
        picked = lax.dot_general(
            selector,
            tokens_ref[:, cols],
            (((0,), (0,)), ((), ())),
            preferred_element_type=jnp.float32,
        ).astype(jnp.bfloat16)
        outgoing[:, :, cols] = picked.reshape(n_major, cap, tile)

    rows_in[e, s] = outgoing[e]
    pl.semaphore_wait(barrier, len(partners))

    def remote(src, dst, send, recv, plane, sub):
        return pltpu.make_async_remote_copy(
            src_ref=src,
            dst_ref=dst,
            send_sem=send,
            recv_sem=recv,
            device_id={"ep": plane, "sub": sub},
            device_id_type=MESH,
        )

    sent = []

    def launch(copy):
        copy.start()
        sent.append(copy)

    def spread(k):
        own = rows_in.at[planes[k], s]
        launch(remote(own, own, dx_send.at[k], dx_recv.at[k], e, s_x))
        launch(remote(own, own, dc_send.at[k, 0], dc_recv.at[k, 0], e, s_core))

    def arrived(dst, send, recv):
        remote(dst, dst, send, recv, e, s_x).wait_recv()

    spread(0)
    for k in range(1, n_major):
        launch(
            remote(
                outgoing.at[planes[k]],
                rows_in.at[e, s],
                dz_send.at[k],
                dz_recv.at[k],
                planes[k],
                s,
            )
        )

    def compute(k):
        plane = planes[k]
        if k == 0:
            loads[0].wait()
            loads[1].wait()
        gate_acc[...] = jnp.zeros_like(gate_acc)
        up_acc[...] = jnp.zeros_like(up_acc)

        @pl.loop(0, width // tile)
        def _(j):
            cols = pl.ds(pl.multiple_of(j * tile, tile), tile)
            part = rows_in[plane, :, :, cols].reshape(chunk, tile)
            gate_acc[...] += jnp.dot(part, gate_w[cols, :], preferred_element_type=jnp.float32)
            up_acc[...] += jnp.dot(part, up_w[cols, :], preferred_element_type=jnp.float32)

        gate = gate_acc[...]
        hidden = (jax.nn.silu(gate) * up_acc[...]).astype(jnp.bfloat16)
        if k == 0:
            loads[2].wait()

        @pl.loop(0, width // tile)
        def _(j):
            cols = pl.ds(pl.multiple_of(j * tile, tile), tile)
            product = jnp.dot(hidden, down_w[:, cols], preferred_element_type=jnp.float32)
            partial[k, :, :, cols] = product.astype(jnp.bfloat16).reshape(4, cap, tile)

        for column in range(2):
            launch(
                remote(
                    partial.at[k, 2 * column + (1 - c)],
                    core_in.at[k, column],
                    rc_send.at[k, column],
                    rc_recv.at[k, column],
                    e,
                    s_core,
                )
            )

    def core_sum(k):
        for column in range(2):
            arrived(core_in.at[k, column], rc_send.at[k, column], rc_recv.at[k, column])
        total = partial[k, s_x].astype(jnp.float32) + core_in[k, 1 - x].astype(jnp.float32)
        x_out[k] = total.astype(jnp.bfloat16)
        launch(remote(x_out.at[k], x_in.at[k], rx_send.at[k], rx_recv.at[k], e, s_x))

    def x_sum(k):
        arrived(x_in.at[k], rx_send.at[k], rx_recv.at[k])
        total = (
            partial[k, s].astype(jnp.float32)
            + core_in[k, x].astype(jnp.float32)
            + x_in[k].astype(jnp.float32)
        ).astype(jnp.bfloat16)
        if k == 0:
            returned[e] = total
        else:
            z_out[k] = total
            launch(
                remote(
                    z_out.at[k], returned.at[e], rz_send.at[k], rz_recv.at[k], planes[k], s
                )
            )

    for k in range(n_major):
        if k + 1 < n_major:
            arrived(rows_in.at[planes[k + 1], s], dz_send.at[k + 1], dz_recv.at[k + 1])
            spread(k + 1)
        far = rows_in.at[planes[k], s_x]
        arrived(far, dx_send.at[k], dx_recv.at[k])
        launch(remote(far, far, dc_send.at[k, 1], dc_recv.at[k, 1], e, s_core))
        arrived(rows_in.at[planes[k], s_core], dc_send.at[k, 0], dc_recv.at[k, 0])
        arrived(rows_in.at[planes[k], s_far], dc_send.at[k, 1], dc_recv.at[k, 1])
        compute(k)
        if k >= 1:
            x_sum(k - 1)
        core_sum(k)
    x_sum(n_major - 1)

    factor = jnp.sum(
        jnp.where(routes_ref[...] < n_major, weights_ref[...], 0.0), axis=1, keepdims=True
    )
    for k in range(1, n_major):
        arrived(returned.at[planes[k]], rz_send.at[k], rz_recv.at[k])

    @pl.loop(0, width // tile)
    def _(j):
        cols = pl.ds(pl.multiple_of(j * tile, tile), tile)
        picked = jnp.dot(
            selector,
            returned[:, :, cols].reshape(slots, tile),
            preferred_element_type=jnp.float32,
        )
        out_ref[:, cols] = (factor * picked).astype(jnp.bfloat16)

    for copy in sent:
        copy.wait_send()


def fused(tokens, routes, route_weights, w_gate, w_up, w_down):
    rows, width = tokens.shape
    n = lax.axis_size("ep")
    cap = rows // n
    hidden = w_gate.shape[2]
    tile = 1024 if width % 1024 == 0 else 128
    slab = (cap, width)
    bf16 = jnp.bfloat16
    dma = pltpu.SemaphoreType.DMA
    vmem = pl.BlockSpec(memory_space=pltpu.VMEM)
    hbm = pl.BlockSpec(memory_space=pl.ANY)
    return pl.pallas_call(
        functools.partial(layer_kernel, n, cap, tile),
        out_shape=jax.ShapeDtypeStruct((rows, width), bf16),
        in_specs=[vmem, vmem, vmem, hbm, hbm, hbm],
        out_specs=vmem,
        scratch_shapes=[
            pltpu.VMEM((width, hidden), bf16),
            pltpu.VMEM((width, hidden), bf16),
            pltpu.VMEM((hidden, width), bf16),
            pltpu.VMEM((n, *slab), bf16),
            pltpu.VMEM((n, 4, *slab), bf16),
            pltpu.VMEM((n, 4, *slab), bf16),
            pltpu.VMEM((n, 2, *slab), bf16),
            pltpu.VMEM((n, *slab), bf16),
            pltpu.VMEM((n, *slab), bf16),
            pltpu.VMEM((n, *slab), bf16),
            pltpu.VMEM((n, *slab), bf16),
            pltpu.VMEM((4 * cap, hidden), jnp.float32),
            pltpu.VMEM((4 * cap, hidden), jnp.float32),
            dma((3,)),
            dma((n,)),
            dma((n,)),
            dma((n,)),
            dma((n,)),
            dma((n, 2)),
            dma((n, 2)),
            dma((n, 2)),
            dma((n, 2)),
            dma((n,)),
            dma((n,)),
            dma((n,)),
            dma((n,)),
        ],
        compiler_params=pltpu.CompilerParams(
            collective_id=0, has_side_effects=True, vmem_limit_bytes=56 * 1024 * 1024
        ),
        cost_estimate=pl.CostEstimate(
            flops=6 * rows * 4 * width * hidden,
            bytes_accessed=6 * width * hidden,
            transcendentals=rows * 4 * hidden,
        ),
    )(tokens, routes, route_weights, w_gate, w_up, w_down)


def staged(tokens, routes, route_weights, w_gate, w_up, w_down):
    rows, width = tokens.shape
    n_major = lax.axis_size("ep")
    n_minor = lax.axis_size("sub")
    capacity = rows // n_major
    portion_rows = n_major * capacity
    hits = routes[:, :, None] == jnp.arange(n_major, dtype=jnp.int32)[None, None, :]
    chosen = jnp.any(hits, axis=1)
    weight_of = jnp.sum(
        jnp.where(hits, route_weights[:, :, None], jnp.zeros((), jnp.float32)), axis=1
    )
    flags = chosen.astype(jnp.int32)
    slots = jnp.cumsum(flags, axis=0) - flags
    placed = chosen[:, :, None] & (
        slots[:, :, None] == jnp.arange(capacity, dtype=jnp.int32)[None, None, :]
    )
    selector = placed.astype(jnp.bfloat16)
    send_rows = jnp.einsum(
        "rfc,rd->fcd", selector, tokens, preferred_element_type=jnp.float32
    ).astype(jnp.bfloat16)
    came = lax.all_to_all(send_rows, "ep", split_axis=0, concat_axis=0, tiled=True)
    got_rows = lax.all_gather(came.reshape(portion_rows, width), "sub", axis=0, tiled=True)
    gate = jnp.dot(got_rows, w_gate[0], preferred_element_type=jnp.float32)
    up = jnp.dot(got_rows, w_up[0], preferred_element_type=jnp.float32)
    hidden = (jax.nn.silu(gate) * up).astype(jnp.bfloat16)
    mine = lax.psum_scatter(
        jnp.dot(hidden, w_down[0], preferred_element_type=jnp.float32).astype(jnp.bfloat16),
        "sub",
        scatter_dimension=0,
        tiled=True,
    )
    back = mine.reshape(n_major, capacity, width)
    result = lax.all_to_all(back, "ep", split_axis=0, concat_axis=0, tiled=True)
    returned = settle(result).reshape(portion_rows, width)
    picked = jnp.dot(
        selector.reshape(rows, portion_rows), returned, preferred_element_type=jnp.float32
    )
    factor = jnp.sum(weight_of, axis=1)
    return (factor[:, None] * picked).astype(jnp.bfloat16)


def on_device(*args):
    n_major = lax.axis_size("ep")
    rows = args[0].shape[0]
    whole_tiles = rows % n_major == 0 and (rows // n_major) % 16 == 0
    if whole_tiles and lax.axis_size("sub") == 4 and n_major & (n_major - 1) == 0:
        return fused(*args)
    return staged(*args)


def solution(mesh):
    return jax.shard_map(
        on_device,
        mesh=mesh,
        in_specs=(
            P(("groups", "ep", "sub"), None),
            P(("groups", "ep", "sub"), None),
            P(("groups", "ep", "sub"), None),
            P("ep", None, "sub"),
            P("ep", None, "sub"),
            P("ep", "sub", None),
        ),
        out_specs=P(("groups", "ep", "sub"), None),
        check_vma=False,
    )
```

```python
import functools

import jax
import jax.numpy as jnp
from jax import lax
from jax.experimental import pallas as pl
from jax.experimental.pallas import tpu as pltpu
from jax.sharding import PartitionSpec as P

MESH = pl.DeviceIdType.MESH
ORDER = (0, 1, 2, 3)
ISSUE = ((1, 2, 3), (), (), ())


def settle(values):
    return lax.optimization_barrier(values)


def flip(index, step, extent):
    result = 0
    bit = 1
    while bit < extent:
        digit = lax.rem(lax.div(index, bit), 2)
        result = result + (1 - digit if step & bit else digit) * bit
        bit *= 2
    return result


def layer_kernel(
    n_major,
    cap,
    tile,
    tokens_ref,
    routes_ref,
    gate_hbm,
    up_hbm,
    down_hbm,
    returned,
    selector_ref,
    gate_w,
    up_w,
    down_w,
    outgoing,
    rows_in,
    partial,
    core_in,
    x_out,
    x_in,
    z_out,
    gate_acc,
    up_acc,
    w_sem,
    dz_send,
    dz_recv,
    dx_send,
    dx_recv,
    dc_send,
    dc_recv,
    rc_send,
    rc_recv,
    rx_send,
    rx_recv,
    rz_send,
    rz_recv,
):
    rows, width = tokens_ref.shape
    slots = n_major * cap
    chunk = 4 * cap
    e = lax.axis_index("ep")
    s = lax.axis_index("sub")
    x = lax.div(s, 2)
    c = lax.rem(s, 2)
    s_core = 2 * x + (1 - c)
    s_x = 2 * (1 - x) + c
    s_far = 2 * (1 - x) + (1 - c)
    planes = [flip(e, k, n_major) for k in range(n_major)]

    loads = [
        pltpu.make_async_copy(gate_hbm.at[0], gate_w, w_sem.at[0]),
        pltpu.make_async_copy(up_hbm.at[0], up_w, w_sem.at[1]),
        pltpu.make_async_copy(down_hbm.at[0], down_w, w_sem.at[2]),
    ]
    for load in loads:
        load.start()

    barrier = pltpu.get_barrier_semaphore()
    partners = [(planes[k], s) for k in range(1, n_major)] + [(e, s_x), (e, s_core)]
    for plane, sub in partners:
        pl.semaphore_signal(
            barrier, inc=1, device_id={"ep": plane, "sub": sub}, device_id_type=MESH
        )

    slot_row = lax.broadcasted_iota(jnp.int32, (slots, rows), 0)
    expert = lax.div(slot_row, cap)
    place = lax.rem(slot_row, cap)
    chosen = jnp.zeros((slots, rows), jnp.float32)
    for k in range(routes_ref.shape[0]):
        chosen = jnp.maximum(chosen, jnp.where(routes_ref[k : k + 1, :] == expert, 1.0, 0.0))
    earlier = jnp.where(
        lax.broadcasted_iota(jnp.int32, (rows, rows), 0)
        < lax.broadcasted_iota(jnp.int32, (rows, rows), 1),
        1.0,
        0.0,
    ).astype(jnp.bfloat16)
    slot = jnp.dot(chosen.astype(jnp.bfloat16), earlier, preferred_element_type=jnp.float32)
    selector = jnp.where(slot == place.astype(jnp.float32), chosen, 0.0).astype(jnp.bfloat16)
    selector_ref[...] = selector

    @pl.loop(0, width // tile)
    def _(j):
        cols = pl.ds(pl.multiple_of(j * tile, tile), tile)
        picked = jnp.dot(
            selector, tokens_ref[:, cols], preferred_element_type=jnp.float32
        ).astype(jnp.bfloat16)
        outgoing[:, :, cols] = picked.reshape(n_major, cap, tile)

    rows_in[e, s] = outgoing[e]
    pl.semaphore_wait(barrier, len(partners))

    def remote(src, dst, send, recv, plane, sub):
        return pltpu.make_async_remote_copy(
            src_ref=src,
            dst_ref=dst,
            send_sem=send,
            recv_sem=recv,
            device_id={"ep": plane, "sub": sub},
            device_id_type=MESH,
        )

    sent = []

    def launch(copy):
        copy.start()
        sent.append(copy)

    def spread(k):
        own = rows_in.at[planes[k], s]
        launch(remote(own, own, dx_send.at[k], dx_recv.at[k], e, s_x))
        launch(remote(own, own, dc_send.at[k, 0], dc_recv.at[k, 0], e, s_core))

    def arrived(dst, send, recv):
        remote(dst, dst, send, recv, e, s_x).wait_recv()

    def issue(ks):
        for k in ks:
            launch(
                remote(
                    outgoing.at[planes[k]],
                    rows_in.at[e, s],
                    dz_send.at[k],
                    dz_recv.at[k],
                    planes[k],
                    s,
                )
            )

    order = ORDER if n_major == 4 else tuple(range(n_major))
    plan = ISSUE if n_major == 4 else (order[1:],) + ((),) * (n_major - 1)
    issue(plan[0])
    spread(0)

    def compute(k):
        plane = planes[k]
        if k == 0:
            loads[0].wait()
            loads[1].wait()
        gate_acc[...] = jnp.zeros_like(gate_acc)
        up_acc[...] = jnp.zeros_like(up_acc)

        @pl.loop(0, width // tile)
        def _(j):
            cols = pl.ds(pl.multiple_of(j * tile, tile), tile)
            part = rows_in[plane, :, :, cols].reshape(chunk, tile)
            gate_acc[...] += jnp.dot(part, gate_w[cols, :], preferred_element_type=jnp.float32)
            up_acc[...] += jnp.dot(part, up_w[cols, :], preferred_element_type=jnp.float32)

        gate = gate_acc[...]
        hidden = (jax.nn.silu(gate) * up_acc[...]).astype(jnp.bfloat16)
        if k == 0:
            loads[2].wait()

        @pl.loop(0, width // tile)
        def _(j):
            cols = pl.ds(pl.multiple_of(j * tile, tile), tile)
            product = jnp.dot(hidden, down_w[:, cols], preferred_element_type=jnp.float32)
            partial[k, :, :, cols] = product.astype(jnp.bfloat16).reshape(4, cap, tile)

        for column in range(2):
            launch(
                remote(
                    partial.at[k, 2 * column + (1 - c)],
                    core_in.at[k, column],
                    rc_send.at[k, column],
                    rc_recv.at[k, column],
                    e,
                    s_core,
                )
            )

    def core_sum(k):
        for column in range(2):
            arrived(core_in.at[k, column], rc_send.at[k, column], rc_recv.at[k, column])
        total = partial[k, s_x].astype(jnp.float32) + core_in[k, 1 - x].astype(jnp.float32)
        x_out[k] = total.astype(jnp.bfloat16)
        launch(remote(x_out.at[k], x_in.at[k], rx_send.at[k], rx_recv.at[k], e, s_x))

    def x_sum(k):
        arrived(x_in.at[k], rx_send.at[k], rx_recv.at[k])
        total = (
            partial[k, s].astype(jnp.float32)
            + core_in[k, x].astype(jnp.float32)
            + x_in[k].astype(jnp.float32)
        ).astype(jnp.bfloat16)
        if k == 0:
            returned[e] = total
        else:
            z_out[k] = total
            launch(
                remote(
                    z_out.at[k], returned.at[e], rz_send.at[k], rz_recv.at[k], planes[k], s
                )
            )

    for i, k in enumerate(order):
        if i + 1 < n_major:
            later = order[i + 1]
            arrived(rows_in.at[planes[later], s], dz_send.at[later], dz_recv.at[later])
            issue(plan[i + 1])
            spread(later)
        far = rows_in.at[planes[k], s_x]
        arrived(far, dx_send.at[k], dx_recv.at[k])
        launch(remote(far, far, dc_send.at[k, 1], dc_recv.at[k, 1], e, s_core))
        arrived(rows_in.at[planes[k], s_core], dc_send.at[k, 0], dc_recv.at[k, 0])
        arrived(rows_in.at[planes[k], s_far], dc_send.at[k, 1], dc_recv.at[k, 1])
        compute(k)
        if i >= 1:
            x_sum(order[i - 1])
        core_sum(k)
    x_sum(order[-1])

    for k in order[1:]:
        arrived(returned.at[planes[k]], rz_send.at[k], rz_recv.at[k])
    for copy in sent:
        copy.wait_send()


def fused(tokens, routes, route_weights, w_gate, w_up, w_down):
    rows, width = tokens.shape
    n = lax.axis_size("ep")
    cap = rows // n
    hidden = w_gate.shape[2]
    tile = 1024 if width % 1024 == 0 else 128
    slab = (cap, width)
    bf16 = jnp.bfloat16
    dma = pltpu.SemaphoreType.DMA
    vmem = pl.BlockSpec(memory_space=pltpu.VMEM)
    hbm = pl.BlockSpec(memory_space=pl.ANY)
    returned, selector = pl.pallas_call(
        functools.partial(layer_kernel, n, cap, tile),
        out_shape=(
            jax.ShapeDtypeStruct((n, *slab), bf16),
            jax.ShapeDtypeStruct((n * cap, rows), bf16),
        ),
        in_specs=[vmem, vmem, hbm, hbm, hbm],
        out_specs=(vmem, vmem),
        scratch_shapes=[
            pltpu.VMEM((width, hidden), bf16),
            pltpu.VMEM((width, hidden), bf16),
            pltpu.VMEM((hidden, width), bf16),
            pltpu.VMEM((n, *slab), bf16),
            pltpu.VMEM((n, 4, *slab), bf16),
            pltpu.VMEM((n, 4, *slab), bf16),
            pltpu.VMEM((n, 2, *slab), bf16),
            pltpu.VMEM((n, *slab), bf16),
            pltpu.VMEM((n, *slab), bf16),
            pltpu.VMEM((n, *slab), bf16),
            pltpu.VMEM((4 * cap, hidden), jnp.float32),
            pltpu.VMEM((4 * cap, hidden), jnp.float32),
            dma((3,)),
            dma((n,)),
            dma((n,)),
            dma((n,)),
            dma((n,)),
            dma((n, 2)),
            dma((n, 2)),
            dma((n, 2)),
            dma((n, 2)),
            dma((n,)),
            dma((n,)),
            dma((n,)),
            dma((n,)),
        ],
        compiler_params=pltpu.CompilerParams(
            collective_id=0, has_side_effects=True, vmem_limit_bytes=56 * 1024 * 1024
        ),
        cost_estimate=pl.CostEstimate(
            flops=6 * rows * 4 * width * hidden,
            bytes_accessed=6 * width * hidden,
            transcendentals=rows * 4 * hidden,
        ),
    )(tokens, routes.T, w_gate, w_up, w_down)
    factor = jnp.sum(jnp.where(routes < n, route_weights, 0.0), axis=1)
    picked = lax.dot_general(
        selector,
        returned.reshape(n * cap, width),
        (((0,), (0,)), ((), ())),
        preferred_element_type=jnp.float32,
    )
    return (factor[:, None] * picked).astype(bf16)


def staged(tokens, routes, route_weights, w_gate, w_up, w_down):
    rows, width = tokens.shape
    n_major = lax.axis_size("ep")
    n_minor = lax.axis_size("sub")
    capacity = rows // n_major
    portion_rows = n_major * capacity
    hits = routes[:, :, None] == jnp.arange(n_major, dtype=jnp.int32)[None, None, :]
    chosen = jnp.any(hits, axis=1)
    weight_of = jnp.sum(
        jnp.where(hits, route_weights[:, :, None], jnp.zeros((), jnp.float32)), axis=1
    )
    flags = chosen.astype(jnp.int32)
    slots = jnp.cumsum(flags, axis=0) - flags
    placed = chosen[:, :, None] & (
        slots[:, :, None] == jnp.arange(capacity, dtype=jnp.int32)[None, None, :]
    )
    selector = placed.astype(jnp.bfloat16)
    send_rows = jnp.einsum(
        "rfc,rd->fcd", selector, tokens, preferred_element_type=jnp.float32
    ).astype(jnp.bfloat16)
    came = lax.all_to_all(send_rows, "ep", split_axis=0, concat_axis=0, tiled=True)
    got_rows = lax.all_gather(came.reshape(portion_rows, width), "sub", axis=0, tiled=True)
    gate = jnp.dot(got_rows, w_gate[0], preferred_element_type=jnp.float32)
    up = jnp.dot(got_rows, w_up[0], preferred_element_type=jnp.float32)
    hidden = (jax.nn.silu(gate) * up).astype(jnp.bfloat16)
    mine = lax.psum_scatter(
        jnp.dot(hidden, w_down[0], preferred_element_type=jnp.float32).astype(jnp.bfloat16),
        "sub",
        scatter_dimension=0,
        tiled=True,
    )
    back = mine.reshape(n_major, capacity, width)
    result = lax.all_to_all(back, "ep", split_axis=0, concat_axis=0, tiled=True)
    returned = settle(result).reshape(portion_rows, width)
    picked = jnp.dot(
        selector.reshape(rows, portion_rows), returned, preferred_element_type=jnp.float32
    )
    factor = jnp.sum(weight_of, axis=1)
    return (factor[:, None] * picked).astype(jnp.bfloat16)


def on_device(*args):
    n_major = lax.axis_size("ep")
    rows = args[0].shape[0]
    whole_tiles = rows % n_major == 0 and (rows // n_major) % 16 == 0
    if whole_tiles and lax.axis_size("sub") == 4 and n_major & (n_major - 1) == 0:
        return fused(*args)
    return staged(*args)


def solution(mesh):
    return jax.shard_map(
        on_device,
        mesh=mesh,
        in_specs=(
            P(("groups", "ep", "sub"), None),
            P(("groups", "ep", "sub"), None),
            P(("groups", "ep", "sub"), None),
            P("ep", None, "sub"),
            P("ep", None, "sub"),
            P("ep", "sub", None),
        ),
        out_specs=P(("groups", "ep", "sub"), None),
        check_vma=False,
    )
```

```python
import functools

import jax
import jax.numpy as jnp
from jax import lax
from jax.experimental import pallas as pl
from jax.experimental.pallas import tpu as pltpu
from jax.sharding import PartitionSpec as P

MESH = pl.DeviceIdType.MESH
STEPS = (
    *("Z1", "R0", "C0", "Z2", "R1", "C1", "S1"),
    *("Z3", "R2", "C2", "X1", "S2", "R3", "C3"),
    *("X2", "S3", "S0", "X3", "X0"),
)


def settle(values):
    return lax.optimization_barrier(values)


def flip(index, step, extent):
    result = 0
    bit = 1
    while bit < extent:
        digit = lax.rem(lax.div(index, bit), 2)
        result = result + (1 - digit if step & bit else digit) * bit
        bit *= 2
    return result


def layer_kernel(
    n_major,
    cap,
    tile,
    tokens_ref,
    routes_ref,
    gate_hbm,
    up_hbm,
    down_hbm,
    returned,
    selector_ref,
    gate_w,
    up_w,
    down_w,
    outgoing,
    rows_in,
    partial,
    core_in,
    x_out,
    x_in,
    z_out,
    gate_acc,
    up_acc,
    w_sem,
    dz_send,
    dz_recv,
    dx_send,
    dx_recv,
    dc_send,
    dc_recv,
    rc_send,
    rc_recv,
    rx_send,
    rx_recv,
    rz_send,
    rz_recv,
):
    rows, width = tokens_ref.shape
    slots = n_major * cap
    chunk = 4 * cap
    e = lax.axis_index("ep")
    s = lax.axis_index("sub")
    x = lax.div(s, 2)
    c = lax.rem(s, 2)
    s_core = 2 * x + (1 - c)
    s_x = 2 * (1 - x) + c
    s_far = 2 * (1 - x) + (1 - c)
    planes = [flip(e, k, n_major) for k in range(n_major)]

    loads = [
        pltpu.make_async_copy(gate_hbm.at[0], gate_w, w_sem.at[0]),
        pltpu.make_async_copy(up_hbm.at[0], up_w, w_sem.at[1]),
        pltpu.make_async_copy(down_hbm.at[0], down_w, w_sem.at[2]),
    ]
    for load in loads:
        load.start()

    barrier = pltpu.get_barrier_semaphore()
    partners = [(planes[k], s) for k in range(1, n_major)] + [(e, s_x), (e, s_core)]
    for plane, sub in partners:
        pl.semaphore_signal(
            barrier, inc=1, device_id={"ep": plane, "sub": sub}, device_id_type=MESH
        )

    slot_row = lax.broadcasted_iota(jnp.int32, (slots, rows), 0)
    expert = lax.div(slot_row, cap)
    place = lax.rem(slot_row, cap)
    chosen = jnp.zeros((slots, rows), jnp.float32)
    for k in range(routes_ref.shape[0]):
        chosen = jnp.maximum(chosen, jnp.where(routes_ref[k : k + 1, :] == expert, 1.0, 0.0))
    earlier = jnp.where(
        lax.broadcasted_iota(jnp.int32, (rows, rows), 0)
        < lax.broadcasted_iota(jnp.int32, (rows, rows), 1),
        1.0,
        0.0,
    ).astype(jnp.bfloat16)
    slot = jnp.dot(chosen.astype(jnp.bfloat16), earlier, preferred_element_type=jnp.float32)
    selector = jnp.where(slot == place.astype(jnp.float32), chosen, 0.0).astype(jnp.bfloat16)
    selector_ref[...] = selector

    @pl.loop(0, width // tile)
    def _(j):
        cols = pl.ds(pl.multiple_of(j * tile, tile), tile)
        picked = jnp.dot(
            selector, tokens_ref[:, cols], preferred_element_type=jnp.float32
        ).astype(jnp.bfloat16)
        outgoing[:, :, cols] = picked.reshape(n_major, cap, tile)

    rows_in[e, s] = outgoing[e]
    pl.semaphore_wait(barrier, len(partners))

    def remote(src, dst, send, recv, plane, sub):
        return pltpu.make_async_remote_copy(
            src_ref=src,
            dst_ref=dst,
            send_sem=send,
            recv_sem=recv,
            device_id={"ep": plane, "sub": sub},
            device_id_type=MESH,
        )

    sent = []

    def launch(copy):
        copy.start()
        sent.append(copy)

    def spread(k):
        own = rows_in.at[planes[k], s]
        launch(remote(own, own, dx_send.at[k], dx_recv.at[k], e, s_x))
        launch(remote(own, own, dc_send.at[k, 0], dc_recv.at[k, 0], e, s_core))

    def arrived(dst, send, recv):
        remote(dst, dst, send, recv, e, s_x).wait_recv()

    for k in range(1, n_major):
        launch(
            remote(
                outgoing.at[planes[k]],
                rows_in.at[e, s],
                dz_send.at[k],
                dz_recv.at[k],
                planes[k],
                s,
            )
        )
    spread(0)

    def compute(k):
        plane = planes[k]
        if k == 0:
            loads[0].wait()
            loads[1].wait()
        gate_acc[...] = jnp.zeros_like(gate_acc)
        up_acc[...] = jnp.zeros_like(up_acc)

        @pl.loop(0, width // tile)
        def _(j):
            cols = pl.ds(pl.multiple_of(j * tile, tile), tile)
            part = rows_in[plane, :, :, cols].reshape(chunk, tile)
            gate_acc[...] += jnp.dot(part, gate_w[cols, :], preferred_element_type=jnp.float32)
            up_acc[...] += jnp.dot(part, up_w[cols, :], preferred_element_type=jnp.float32)

        gate = gate_acc[...]
        hidden = (jax.nn.silu(gate) * up_acc[...]).astype(jnp.bfloat16)
        if k == 0:
            loads[2].wait()

        @pl.loop(0, width // tile)
        def _(j):
            cols = pl.ds(pl.multiple_of(j * tile, tile), tile)
            product = jnp.dot(hidden, down_w[:, cols], preferred_element_type=jnp.float32)
            partial[k, :, :, cols] = product.astype(jnp.bfloat16).reshape(4, cap, tile)

        for column in range(2):
            launch(
                remote(
                    partial.at[k, 2 * column + (1 - c)],
                    core_in.at[k, column],
                    rc_send.at[k, column],
                    rc_recv.at[k, column],
                    e,
                    s_core,
                )
            )

    def core_sum(k):
        for column in range(2):
            arrived(core_in.at[k, column], rc_send.at[k, column], rc_recv.at[k, column])
        total = partial[k, s_x].astype(jnp.float32) + core_in[k, 1 - x].astype(jnp.float32)
        x_out[k] = total.astype(jnp.bfloat16)
        launch(remote(x_out.at[k], x_in.at[k], rx_send.at[k], rx_recv.at[k], e, s_x))

    def x_sum(k):
        arrived(x_in.at[k], rx_send.at[k], rx_recv.at[k])
        total = (
            partial[k, s].astype(jnp.float32)
            + core_in[k, x].astype(jnp.float32)
            + x_in[k].astype(jnp.float32)
        ).astype(jnp.bfloat16)
        if k == 0:
            returned[e] = total
        else:
            z_out[k] = total
            launch(
                remote(
                    z_out.at[k], returned.at[e], rz_send.at[k], rz_recv.at[k], planes[k], s
                )
            )

    def bring(k):
        arrived(rows_in.at[planes[k], s], dz_send.at[k], dz_recv.at[k])
        spread(k)

    def relay(k):
        far = rows_in.at[planes[k], s_x]
        arrived(far, dx_send.at[k], dx_recv.at[k])
        launch(remote(far, far, dc_send.at[k, 1], dc_recv.at[k, 1], e, s_core))

    def work(k):
        arrived(rows_in.at[planes[k], s_core], dc_send.at[k, 0], dc_recv.at[k, 0])
        arrived(rows_in.at[planes[k], s_far], dc_send.at[k, 1], dc_recv.at[k, 1])
        compute(k)

    does = {"Z": bring, "R": relay, "C": work, "S": core_sum, "X": x_sum}
    for step in STEPS:
        does[step[0]](int(step[1]))

    for k in range(1, n_major):
        arrived(returned.at[planes[k]], rz_send.at[k], rz_recv.at[k])

    for copy in sent:
        copy.wait_send()


def fused(tokens, routes, route_weights, w_gate, w_up, w_down):
    rows, width = tokens.shape
    n = lax.axis_size("ep")
    cap = rows // n
    hidden = w_gate.shape[2]
    tile = 1024 if width % 1024 == 0 else 128
    slab = (cap, width)
    bf16 = jnp.bfloat16
    dma = pltpu.SemaphoreType.DMA
    vmem = pl.BlockSpec(memory_space=pltpu.VMEM)
    hbm = pl.BlockSpec(memory_space=pl.ANY)
    returned, selector = pl.pallas_call(
        functools.partial(layer_kernel, n, cap, tile),
        out_shape=(
            jax.ShapeDtypeStruct((n, *slab), bf16),
            jax.ShapeDtypeStruct((n * cap, rows), bf16),
        ),
        in_specs=[vmem, vmem, hbm, hbm, hbm],
        out_specs=(vmem, vmem),
        scratch_shapes=[
            pltpu.VMEM((width, hidden), bf16),
            pltpu.VMEM((width, hidden), bf16),
            pltpu.VMEM((hidden, width), bf16),
            pltpu.VMEM((n, *slab), bf16),
            pltpu.VMEM((n, 4, *slab), bf16),
            pltpu.VMEM((n, 4, *slab), bf16),
            pltpu.VMEM((n, 2, *slab), bf16),
            pltpu.VMEM((n, *slab), bf16),
            pltpu.VMEM((n, *slab), bf16),
            pltpu.VMEM((n, *slab), bf16),
            pltpu.VMEM((4 * cap, hidden), jnp.float32),
            pltpu.VMEM((4 * cap, hidden), jnp.float32),
            dma((3,)),
            dma((n,)),
            dma((n,)),
            dma((n,)),
            dma((n,)),
            dma((n, 2)),
            dma((n, 2)),
            dma((n, 2)),
            dma((n, 2)),
            dma((n,)),
            dma((n,)),
            dma((n,)),
            dma((n,)),
        ],
        compiler_params=pltpu.CompilerParams(
            collective_id=0, has_side_effects=True, vmem_limit_bytes=56 * 1024 * 1024
        ),
        cost_estimate=pl.CostEstimate(
            flops=6 * rows * 4 * width * hidden,
            bytes_accessed=6 * width * hidden,
            transcendentals=rows * 4 * hidden,
        ),
    )(tokens, routes.T, w_gate, w_up, w_down)
    factor = jnp.sum(jnp.where(routes < n, route_weights, 0.0), axis=1)
    picked = lax.dot_general(
        selector,
        returned.reshape(n * cap, width),
        (((0,), (0,)), ((), ())),
        preferred_element_type=jnp.float32,
    )
    return (factor[:, None] * picked).astype(bf16)


def staged(tokens, routes, route_weights, w_gate, w_up, w_down):
    rows, width = tokens.shape
    n_major = lax.axis_size("ep")
    n_minor = lax.axis_size("sub")
    capacity = rows // n_major
    portion_rows = n_major * capacity
    hits = routes[:, :, None] == jnp.arange(n_major, dtype=jnp.int32)[None, None, :]
    chosen = jnp.any(hits, axis=1)
    weight_of = jnp.sum(
        jnp.where(hits, route_weights[:, :, None], jnp.zeros((), jnp.float32)), axis=1
    )
    flags = chosen.astype(jnp.int32)
    slots = jnp.cumsum(flags, axis=0) - flags
    placed = chosen[:, :, None] & (
        slots[:, :, None] == jnp.arange(capacity, dtype=jnp.int32)[None, None, :]
    )
    selector = placed.astype(jnp.bfloat16)
    send_rows = jnp.einsum(
        "rfc,rd->fcd", selector, tokens, preferred_element_type=jnp.float32
    ).astype(jnp.bfloat16)
    came = lax.all_to_all(send_rows, "ep", split_axis=0, concat_axis=0, tiled=True)
    got_rows = lax.all_gather(came.reshape(portion_rows, width), "sub", axis=0, tiled=True)
    gate = jnp.dot(got_rows, w_gate[0], preferred_element_type=jnp.float32)
    up = jnp.dot(got_rows, w_up[0], preferred_element_type=jnp.float32)
    hidden = (jax.nn.silu(gate) * up).astype(jnp.bfloat16)
    mine = lax.psum_scatter(
        jnp.dot(hidden, w_down[0], preferred_element_type=jnp.float32).astype(jnp.bfloat16),
        "sub",
        scatter_dimension=0,
        tiled=True,
    )
    back = mine.reshape(n_major, capacity, width)
    result = lax.all_to_all(back, "ep", split_axis=0, concat_axis=0, tiled=True)
    returned = settle(result).reshape(portion_rows, width)
    picked = jnp.dot(
        selector.reshape(rows, portion_rows), returned, preferred_element_type=jnp.float32
    )
    factor = jnp.sum(weight_of, axis=1)
    return (factor[:, None] * picked).astype(jnp.bfloat16)


def on_device(*args):
    n_major = lax.axis_size("ep")
    rows = args[0].shape[0]
    whole_tiles = rows % n_major == 0 and (rows // n_major) % 16 == 0
    if whole_tiles and lax.axis_size("sub") == 4 and n_major == 4:
        return fused(*args)
    return staged(*args)


def solution(mesh):
    return jax.shard_map(
        on_device,
        mesh=mesh,
        in_specs=(
            P(("groups", "ep", "sub"), None),
            P(("groups", "ep", "sub"), None),
            P(("groups", "ep", "sub"), None),
            P("ep", None, "sub"),
            P("ep", None, "sub"),
            P("ep", "sub", None),
        ),
        out_specs=P(("groups", "ep", "sub"), None),
        check_vma=False,
    )
```

```python
import functools

import jax
import jax.numpy as jnp
from jax import lax
from jax.experimental import pallas as pl
from jax.experimental.pallas import tpu as pltpu
from jax.sharding import PartitionSpec as P

MESH = pl.DeviceIdType.MESH
STEPS = (
    *("Z1", "R0", "C0", "Z2", "R1", "C1", "S1"),
    *("Z3", "R2", "C2", "X1", "S2", "R3", "C3"),
    *("X2", "S3", "S0", "X3", "X0"),
)


def settle(values):
    return lax.optimization_barrier(values)


def flip(index, step, extent):
    result = 0
    bit = 1
    while bit < extent:
        digit = lax.rem(lax.div(index, bit), 2)
        result = result + (1 - digit if step & bit else digit) * bit
        bit *= 2
    return result


def layer_kernel(
    n_major,
    cap,
    tile,
    tokens_ref,
    routes_ref,
    gate_hbm,
    up_hbm,
    down_hbm,
    returned,
    selector_ref,
    gate_w,
    up_w,
    down_w,
    outgoing,
    rows_in,
    partial,
    core_in,
    x_out,
    x_in,
    z_out,
    gate_acc,
    up_acc,
    w_sem,
    dz_send,
    dz_recv,
    dx_send,
    dx_recv,
    dc_send,
    dc_recv,
    rc_send,
    rc_recv,
    rx_send,
    rx_recv,
    rz_send,
    rz_recv,
):
    rows, width = tokens_ref.shape
    slots = n_major * cap
    chunk = 4 * cap
    e = lax.axis_index("ep")
    s = lax.axis_index("sub")
    x = lax.div(s, 2)
    c = lax.rem(s, 2)
    s_core = 2 * x + (1 - c)
    s_x = 2 * (1 - x) + c
    s_far = 2 * (1 - x) + (1 - c)
    planes = [flip(e, k, n_major) for k in range(n_major)]

    loads = [
        pltpu.make_async_copy(gate_hbm.at[0], gate_w, w_sem.at[0]),
        pltpu.make_async_copy(up_hbm.at[0], up_w, w_sem.at[1]),
        pltpu.make_async_copy(down_hbm.at[0], down_w, w_sem.at[2]),
    ]
    for load in loads:
        load.start()

    barrier = pltpu.get_barrier_semaphore()
    partners = [(planes[k], s) for k in range(1, n_major)] + [(e, s_x), (e, s_core)]
    for plane, sub in partners:
        pl.semaphore_signal(
            barrier, inc=1, device_id={"ep": plane, "sub": sub}, device_id_type=MESH
        )

    slot_row = lax.broadcasted_iota(jnp.int32, (slots, rows), 0)
    expert = lax.div(slot_row, cap)
    place = lax.rem(slot_row, cap)
    chosen = jnp.zeros((slots, rows), jnp.float32)
    for k in range(routes_ref.shape[0]):
        chosen = jnp.maximum(chosen, jnp.where(routes_ref[k : k + 1, :] == expert, 1.0, 0.0))
    earlier = jnp.where(
        lax.broadcasted_iota(jnp.int32, (rows, rows), 0)
        < lax.broadcasted_iota(jnp.int32, (rows, rows), 1),
        1.0,
        0.0,
    ).astype(jnp.bfloat16)
    slot = jnp.dot(chosen.astype(jnp.bfloat16), earlier, preferred_element_type=jnp.float32)
    selector = jnp.where(slot == place.astype(jnp.float32), chosen, 0.0).astype(jnp.bfloat16)
    selector_ref[...] = selector

    @pl.loop(0, width // tile)
    def _(j):
        cols = pl.ds(pl.multiple_of(j * tile, tile), tile)
        picked = jnp.dot(
            selector, tokens_ref[:, cols], preferred_element_type=jnp.float32
        ).astype(jnp.bfloat16)
        outgoing[:, :, cols] = picked.reshape(n_major, cap, tile)

    rows_in[e, s] = outgoing[e]
    pl.semaphore_wait(barrier, len(partners))

    def remote(src, dst, send, recv, plane, sub):
        return pltpu.make_async_remote_copy(
            src_ref=src,
            dst_ref=dst,
            send_sem=send,
            recv_sem=recv,
            device_id={"ep": plane, "sub": sub},
            device_id_type=MESH,
        )

    sent = []

    def launch(copy):
        copy.start()
        sent.append(copy)

    def spread(k):
        own = rows_in.at[planes[k], s]
        launch(remote(own, own, dx_send.at[k], dx_recv.at[k], e, s_x))
        launch(remote(own, own, dc_send.at[k, 0], dc_recv.at[k, 0], e, s_core))

    def arrived(dst, send, recv):
        remote(dst, dst, send, recv, e, s_x).wait_recv()

    spread(0)
    for k in range(1, n_major):
        launch(
            remote(
                outgoing.at[planes[k]],
                rows_in.at[e, s],
                dz_send.at[k],
                dz_recv.at[k],
                planes[k],
                s,
            )
        )

    def compute(k):
        plane = planes[k]
        if k == 0:
            loads[0].wait()
            loads[1].wait()
        gate_acc[...] = jnp.zeros_like(gate_acc)
        up_acc[...] = jnp.zeros_like(up_acc)

        @pl.loop(0, width // tile)
        def _(j):
            cols = pl.ds(pl.multiple_of(j * tile, tile), tile)
            part = rows_in[plane, :, :, cols].reshape(chunk, tile)
            gate_acc[...] += jnp.dot(part, gate_w[cols, :], preferred_element_type=jnp.float32)
            up_acc[...] += jnp.dot(part, up_w[cols, :], preferred_element_type=jnp.float32)

        gate = gate_acc[...]
        hidden = (jax.nn.silu(gate) * up_acc[...]).astype(jnp.bfloat16)
        if k == 0:
            loads[2].wait()

        @pl.loop(0, width // tile)
        def _(j):
            cols = pl.ds(pl.multiple_of(j * tile, tile), tile)
            product = jnp.dot(hidden, down_w[:, cols], preferred_element_type=jnp.float32)
            partial[k, :, :, cols] = product.astype(jnp.bfloat16).reshape(4, cap, tile)

        for column in range(2):
            launch(
                remote(
                    partial.at[k, 2 * column + (1 - c)],
                    core_in.at[k, column],
                    rc_send.at[k, column],
                    rc_recv.at[k, column],
                    e,
                    s_core,
                )
            )

    def core_sum(k):
        for column in range(2):
            arrived(core_in.at[k, column], rc_send.at[k, column], rc_recv.at[k, column])
        total = partial[k, s_x].astype(jnp.float32) + core_in[k, 1 - x].astype(jnp.float32)
        x_out[k] = total.astype(jnp.bfloat16)
        launch(remote(x_out.at[k], x_in.at[k], rx_send.at[k], rx_recv.at[k], e, s_x))

    def x_sum(k):
        arrived(x_in.at[k], rx_send.at[k], rx_recv.at[k])
        total = (
            partial[k, s].astype(jnp.float32)
            + core_in[k, x].astype(jnp.float32)
            + x_in[k].astype(jnp.float32)
        ).astype(jnp.bfloat16)
        if k == 0:
            returned[e] = total
        else:
            z_out[k] = total
            launch(
                remote(
                    z_out.at[k], returned.at[e], rz_send.at[k], rz_recv.at[k], planes[k], s
                )
            )

    def bring(k):
        arrived(rows_in.at[planes[k], s], dz_send.at[k], dz_recv.at[k])
        spread(k)

    def relay(k):
        far = rows_in.at[planes[k], s_x]
        arrived(far, dx_send.at[k], dx_recv.at[k])
        launch(remote(far, far, dc_send.at[k, 1], dc_recv.at[k, 1], e, s_core))

    def work(k):
        arrived(rows_in.at[planes[k], s_core], dc_send.at[k, 0], dc_recv.at[k, 0])
        arrived(rows_in.at[planes[k], s_far], dc_send.at[k, 1], dc_recv.at[k, 1])
        compute(k)

    does = {"Z": bring, "R": relay, "C": work, "S": core_sum, "X": x_sum}
    for step in STEPS:
        does[step[0]](int(step[1]))

    for k in range(1, n_major):
        arrived(returned.at[planes[k]], rz_send.at[k], rz_recv.at[k])

    for copy in sent:
        copy.wait_send()


def fused(tokens, routes, route_weights, w_gate, w_up, w_down):
    rows, width = tokens.shape
    n = lax.axis_size("ep")
    cap = rows // n
    hidden = w_gate.shape[2]
    tile = 1024 if width % 1024 == 0 else 128
    slab = (cap, width)
    bf16 = jnp.bfloat16
    dma = pltpu.SemaphoreType.DMA
    vmem = pl.BlockSpec(memory_space=pltpu.VMEM)
    hbm = pl.BlockSpec(memory_space=pl.ANY)
    returned, selector = pl.pallas_call(
        functools.partial(layer_kernel, n, cap, tile),
        out_shape=(
            jax.ShapeDtypeStruct((n, *slab), bf16),
            jax.ShapeDtypeStruct((n * cap, rows), bf16),
        ),
        in_specs=[vmem, vmem, hbm, hbm, hbm],
        out_specs=(vmem, vmem),
        scratch_shapes=[
            pltpu.VMEM((width, hidden), bf16),
            pltpu.VMEM((width, hidden), bf16),
            pltpu.VMEM((hidden, width), bf16),
            pltpu.VMEM((n, *slab), bf16),
            pltpu.VMEM((n, 4, *slab), bf16),
            pltpu.VMEM((n, 4, *slab), bf16),
            pltpu.VMEM((n, 2, *slab), bf16),
            pltpu.VMEM((n, *slab), bf16),
            pltpu.VMEM((n, *slab), bf16),
            pltpu.VMEM((n, *slab), bf16),
            pltpu.VMEM((4 * cap, hidden), jnp.float32),
            pltpu.VMEM((4 * cap, hidden), jnp.float32),
            dma((3,)),
            dma((n,)),
            dma((n,)),
            dma((n,)),
            dma((n,)),
            dma((n, 2)),
            dma((n, 2)),
            dma((n, 2)),
            dma((n, 2)),
            dma((n,)),
            dma((n,)),
            dma((n,)),
            dma((n,)),
        ],
        compiler_params=pltpu.CompilerParams(
            collective_id=0, has_side_effects=True, vmem_limit_bytes=56 * 1024 * 1024
        ),
        cost_estimate=pl.CostEstimate(
            flops=6 * rows * 4 * width * hidden,
            bytes_accessed=6 * width * hidden,
            transcendentals=rows * 4 * hidden,
        ),
    )(tokens, routes.T, w_gate, w_up, w_down)
    factor = jnp.sum(jnp.where(routes < n, route_weights, 0.0), axis=1)
    picked = lax.dot_general(
        selector,
        returned.reshape(n * cap, width),
        (((0,), (0,)), ((), ())),
        preferred_element_type=jnp.float32,
    )
    return (factor[:, None] * picked).astype(bf16)


def staged(tokens, routes, route_weights, w_gate, w_up, w_down):
    rows, width = tokens.shape
    n_major = lax.axis_size("ep")
    n_minor = lax.axis_size("sub")
    capacity = rows // n_major
    portion_rows = n_major * capacity
    hits = routes[:, :, None] == jnp.arange(n_major, dtype=jnp.int32)[None, None, :]
    chosen = jnp.any(hits, axis=1)
    weight_of = jnp.sum(
        jnp.where(hits, route_weights[:, :, None], jnp.zeros((), jnp.float32)), axis=1
    )
    flags = chosen.astype(jnp.int32)
    slots = jnp.cumsum(flags, axis=0) - flags
    placed = chosen[:, :, None] & (
        slots[:, :, None] == jnp.arange(capacity, dtype=jnp.int32)[None, None, :]
    )
    selector = placed.astype(jnp.bfloat16)
    send_rows = jnp.einsum(
        "rfc,rd->fcd", selector, tokens, preferred_element_type=jnp.float32
    ).astype(jnp.bfloat16)
    came = lax.all_to_all(send_rows, "ep", split_axis=0, concat_axis=0, tiled=True)
    got_rows = lax.all_gather(came.reshape(portion_rows, width), "sub", axis=0, tiled=True)
    gate = jnp.dot(got_rows, w_gate[0], preferred_element_type=jnp.float32)
    up = jnp.dot(got_rows, w_up[0], preferred_element_type=jnp.float32)
    hidden = (jax.nn.silu(gate) * up).astype(jnp.bfloat16)
    mine = lax.psum_scatter(
        jnp.dot(hidden, w_down[0], preferred_element_type=jnp.float32).astype(jnp.bfloat16),
        "sub",
        scatter_dimension=0,
        tiled=True,
    )
    back = mine.reshape(n_major, capacity, width)
    result = lax.all_to_all(back, "ep", split_axis=0, concat_axis=0, tiled=True)
    returned = settle(result).reshape(portion_rows, width)
    picked = jnp.dot(
        selector.reshape(rows, portion_rows), returned, preferred_element_type=jnp.float32
    )
    factor = jnp.sum(weight_of, axis=1)
    return (factor[:, None] * picked).astype(jnp.bfloat16)


def on_device(*args):
    n_major = lax.axis_size("ep")
    rows = args[0].shape[0]
    whole_tiles = rows % n_major == 0 and (rows // n_major) % 16 == 0
    if whole_tiles and lax.axis_size("sub") == 4 and n_major == 4:
        return fused(*args)
    return staged(*args)


def solution(mesh):
    return jax.shard_map(
        on_device,
        mesh=mesh,
        in_specs=(
            P(("groups", "ep", "sub"), None),
            P(("groups", "ep", "sub"), None),
            P(("groups", "ep", "sub"), None),
            P("ep", None, "sub"),
            P("ep", None, "sub"),
            P("ep", "sub", None),
        ),
        out_specs=P(("groups", "ep", "sub"), None),
        check_vma=False,
    )
```
